32 devices in a mesh: groups: 2 (over y), dp: 4 (over z), cent: 4 (over x, core).
Axes of the slice: x: 2, y: 2, z: 4, core: 2. Of those that a mesh axis runs over, the one named last changes fastest.
Arguments:
- rows: bfloat16 [2048, 1024], P(('groups', 'dp', 'cent')), parts along dimension 0, may hold values from -6 to 6
- coarse_ids: int32 [2048, 4], P(('groups', 'dp', 'cent')), parts along dimension 0, may hold values from 0 to 127, all different within a row; in each aligned block of 64 rows (0 to 63, 64 to 127, ...) at most 4 rows name the same one
- parent: int32 [65536], P('groups'), parts along dimension 0, may hold values from 0 to 127, as said below
- fine_cent: bfloat16 [65536, 1024], P(('groups', 'dp', 'cent')), parts along dimension 0, may hold values from -16 to 16
- coarse_cent: bfloat16 [256, 1024], P('groups'), parts along dimension 0, may hold values from -16 to 16
Outputs:
- fine_out: bfloat16 [65536, 1024], P(('groups', 'dp', 'cent')), parts along dimension 0
- coarse_out: bfloat16 [256, 1024], P('groups'), parts along dimension 0
The draws below stay inside these ranges and needn't reach their ends.
There are 2 independent parts, one for each index of `groups`. The reference program is written for one: setup_inputs(seed, part) draws one part's arguments, and reference() takes and returns one part's arrays. A program takes and returns all parts, laid end to end along the dimension named above; each array names one. Nothing has to cross between parts.
Inputs may be any that keep to these rules, and one draw needn't show every extreme that they name: `coarse_ids`: in each aligned block of 64 rows (the rows of one device) no coarse cluster is named by more than 4 rows, and the ids of one row differ. `parent`: each coarse cluster has exactly 256 children; the fine clusters form 4 * 4 blocks of consecutive indices of equal size, and each block holds all the children of its coarse clusters.
All inputs are finite; a program needn't handle non-finite values.
Results may differ from the reference program's by a relative error of at most 0.0048.
Values may be sent and summed in bfloat16 or wider, within the bound.
A program may use at most 64 MiB of HBM per device.

```python
import math
import jax
import jax.numpy as jnp
import numpy as np
from jax import lax

D = 1024
COARSE = 128
CHILD = 256
TOP = 4
ITERS = 2
ROW_DEV = 64
FINE = 32768
ROWS = 1024
MOST = 4
PRIOR = 8
N_DP = 4
N_CENT = 4


def draw_parent(key, part):
    key = jax.random.fold_in(key, 7)
    owners = N_DP * N_CENT
    per_owner = COARSE // owners
    block_size = per_owner * CHILD
    order_key, block_key = jax.random.split(key)
    coarse_order = jax.random.permutation(order_key, COARSE)
    block_keys = jax.random.split(block_key, owners)
    inner = jax.vmap(lambda k: jax.random.permutation(k, block_size))(block_keys)
    local = inner // CHILD + (jnp.arange(owners) * per_owner)[:, None]
    return coarse_order[local.reshape(-1)].astype(jnp.int32)


def draw_fine_cent(key, part):
    key = jax.random.fold_in(key, 11)
    base_key = jax.random.fold_in(key, 0)
    base = jnp.clip(jax.random.normal(base_key, (FINE, D), jnp.float32), -4.0, 4.0)
    return base.astype(jnp.bfloat16)


def draw_coarse_cent(key, part):
    key = jax.random.fold_in(key, 13)
    base_key = jax.random.fold_in(key, 0)
    base = jnp.clip(jax.random.normal(base_key, (COARSE, D), jnp.float32), -4.0, 4.0)
    return base.astype(jnp.bfloat16)


def with_spikes(values, own_key, source, target, blocks, factor):
    owner, partner = [(jnp.arange(values.shape[axis_at]) // (values.shape[axis_at] // blocks)).reshape([-1 if axis == axis_at else 1 for axis in range(values.ndim)]) for axis_at in (source, target)]
    chosen = jax.random.permutation(own_key, blocks)[partner]
    strong = (owner == chosen) | (owner == (partner + blocks // 2) % blocks)
    return jnp.where(strong, factor * values, values)


def steps_of(stream_key, extent, cuts, low, high):
    factor_of = 1.0
    for dim, shards_of in cuts:
        heights = jax.random.uniform(jax.random.fold_in(jax.random.fold_in(stream_key, 6), dim), (shards_of,), jnp.float32, low / len(cuts), high / len(cuts))
        factor_of = factor_of * jnp.repeat(jnp.exp(heights), extent[dim] // shards_of).reshape((-1,) + (1,) * (len(extent) - 1 - dim))
    return factor_of


def shared_out(stream_key, own, number, rows, count, top, limit, skew):
    order = jax.random.permutation(stream_key, count)
    heavy_load, common = shares(count, rows * top, limit, skew, True), shares(count, rows * top, limit, skew, False)
    places = jnp.arange(count)

    def named(sizes, turn):
        used = int((sizes > 0).sum())
        fixed = max(1, used // 4)
        passed = fixed + (places - fixed + turn * (used - fixed)) % max(1, count - fixed)
        return jnp.zeros((count,), jnp.int32).at[order[jnp.where(places < fixed, places, passed)]].set(jnp.asarray(sizes, jnp.int32))

    sizes = jnp.where(number % 4 == 0, named(heavy_load, number // 4), named(common, number - number // 4 - 1))
    mixed = jax.random.permutation(jax.random.fold_in(own, 3), count)
    giver, sink = mixed[0:count // 2 * 2:2], mixed[1:count // 2 * 2:2]
    room = jnp.minimum(sizes[giver] - 1, limit - sizes[sink]) // 2
    room = jnp.where((giver == order[0]) | (sink == order[0]) | (sizes[sink] == 0), 0, jnp.maximum(room, 0))
    passed = jax.random.randint(jax.random.fold_in(own, 4), (count // 2,), 0, 1 << 20) % (room + 1)
    sizes = sizes.at[giver].add(-passed).at[sink].add(passed)
    items = jnp.searchsorted(jnp.cumsum(sizes), jnp.arange(rows * top), side="right").astype(jnp.int32)
    listing = items.reshape(top, rows).T
    listing = listing[jax.random.permutation(jax.random.fold_in(own, 1), rows)]
    turn = jax.random.randint(jax.random.fold_in(own, 2), (rows, 1), 0, top)
    return jnp.take_along_axis(listing, (jnp.arange(top)[None, :] + turn) % top, axis=1)


def shares(number_of, total, limit, lean, full):
    weights = [(1 << 20) // math.isqrt(rank ** lean) + 1 for rank in range(1, number_of + 1)]
    largest = limit if full else min(limit, max(-(-total // number_of), total * weights[0] // sum(weights)))
    least = 1 if total - largest >= number_of - 1 else 0
    given, surplus = [largest] + [least] * (number_of - 1), total - largest - least * (number_of - 1)
    while surplus > 0:
        free = [i for i in range(1, number_of) if given[i] < largest] or [i for i in range(1, number_of) if given[i] < limit]
        whole, budget = sum([weights[i] for i in free]), surplus
        for i in free:
            addition = min(limit - given[i], max(1, budget * weights[i] // whole), surplus)
            given[i] = given[i] + addition
            surplus = surplus - addition
    return np.array(given)


def heavy_noise(own_key, extent, scale, limit, cuts, heavy, kind=jnp.bfloat16):
    result = scale * jax.random.normal(own_key, extent, jnp.float32)
    if cuts:
        result = result * steps_of(own_key, extent, cuts, -0.22, 0.18)
    return jnp.clip(with_spikes(result, jax.random.fold_in(own_key, 3), *heavy), -limit, limit).astype(kind)


def setup_inputs(seed: int = 0, part: int = 0) -> dict:
    key_of = jax.random.split(jax.random.key(seed), 6)
    part_keys = jax.random.split(jax.random.fold_in(key_of[5], part), 6)
    rows = heavy_noise(part_keys[0], (ROWS, D), 1.0, 6.0, ((0, 16),), (0, 1, 16, 2.0))
    coarse_ids_keys = jax.random.split(jax.random.fold_in(part_keys[1], 1), ROWS // ROW_DEV)
    coarse_ids_turns = jax.random.permutation(jax.random.fold_in(part_keys[1], 3), ROWS // ROW_DEV)
    coarse_ids = jax.vmap(lambda own, number: shared_out(jax.random.fold_in(part_keys[1], 2), own, number, ROW_DEV, COARSE, TOP, MOST, 2))(coarse_ids_keys, coarse_ids_turns).reshape((ROWS, TOP))
    parent = draw_parent(jax.random.fold_in(jax.random.fold_in(key_of[5], part), 71), part)
    fine_cent = draw_fine_cent(jax.random.fold_in(jax.random.fold_in(key_of[5], part), 71), part)
    coarse_cent = draw_coarse_cent(jax.random.fold_in(jax.random.fold_in(key_of[5], part), 71), part)
    return {"rows": rows, "coarse_ids": coarse_ids, "parent": parent, "fine_cent": fine_cent, "coarse_cent": coarse_cent}


def route_tables(parent, block_size):
    fine_index = jnp.arange(parent.shape[0], dtype=jnp.int32)
    owner = jnp.zeros((COARSE,), jnp.int32).at[parent].max((fine_index // block_size).astype(jnp.int32))
    same = owner[:, None] == owner[None, :]
    below = jnp.arange(COARSE, dtype=jnp.int32)[None, :] < jnp.arange(COARSE, dtype=jnp.int32)[:, None]
    local = lax.optimization_barrier(jnp.sum((same & below).astype(jnp.int32), axis=1)).astype(jnp.int32)
    return (owner, local)

def pair_slots(block_ids, owner, local, per_owner):
    flat = block_ids.reshape(-1)
    onehot = (flat[:, None] == jnp.arange(COARSE, dtype=jnp.int32)[None, :]).astype(jnp.int32)
    before = jnp.cumsum(onehot, axis=0) - onehot
    rank = lax.optimization_barrier(jnp.sum(before * onehot, axis=1)).astype(jnp.int32)
    return ((owner[flat] * per_owner + local[flat]) * MOST + rank).astype(jnp.int32)

def coarse_weights(rows, coarse_ids, coarse):
    scale = 1.0 / math.sqrt(D)
    coarse_f = coarse.astype(jnp.float32)
    norms = lax.optimization_barrier(jnp.sum(coarse_f * coarse_f, axis=1))
    dots = jnp.dot(rows, coarse.T, preferred_element_type=jnp.float32)
    full = (dots - 0.5 * norms[None, :]) * scale
    picked = jnp.take_along_axis(full, coarse_ids, axis=1)
    return jax.nn.softmax(picked, axis=1)

def coarse_update(rows, coarse_ids, weights, coarse, prior):
    match = (coarse_ids[:, :, None] == jnp.arange(COARSE, dtype=jnp.int32)[None, None, :]).astype(jnp.float32)
    spread = lax.optimization_barrier(jnp.sum(weights[:, :, None] * match, axis=1))
    spread_b = spread.astype(jnp.bfloat16)
    total = jnp.dot(spread_b.T, rows, preferred_element_type=jnp.float32)
    mass = lax.optimization_barrier(jnp.sum(lax.optimization_barrier(spread_b).astype(jnp.float32), axis=0))
    return ((total + prior * coarse.astype(jnp.float32)) / (mass[:, None] + prior)).astype(jnp.bfloat16)

def owner_update(arrived, arrived_q, sorted_cent):
    scale = 1.0 / math.sqrt(D)
    cent_f = sorted_cent.astype(jnp.float32)
    norms = lax.optimization_barrier(jnp.sum(cent_f * cent_f, axis=-1))
    arrived_f = arrived.astype(jnp.float32)
    dots = jnp.einsum('slmd,lcd->lsmc', arrived_f, cent_f)
    logits = (dots - 0.5 * norms[:, None, None, :]) * scale
    prob = jax.nn.softmax(logits, axis=-1)
    resp = jnp.transpose(arrived_q.astype(jnp.float32), (1, 0, 2))[..., None] * prob
    resp_b = resp.astype(jnp.bfloat16)
    fine_sum = jnp.einsum('lsmc,slmd->lcd', resp_b.astype(jnp.float32), arrived_f)
    mass = lax.optimization_barrier(jnp.sum(resp, axis=(1, 2)))
    return ((fine_sum + cent_f) / (mass[..., None] + 1.0)).astype(jnp.bfloat16)

def reference(rows, coarse_ids, parent, fine_cent, coarse_cent):
    owners = N_DP * N_CENT
    per_owner = COARSE // owners
    block_size = FINE // owners
    width = per_owner * MOST
    owner, local = route_tables(parent, block_size)
    blocks = coarse_ids.reshape(owners, ROW_DEV, TOP)
    slots = jax.vmap(lambda ids: pair_slots(ids, owner, local, per_owner))(blocks)
    pair_row = (jnp.arange(owners, dtype=jnp.int32)[:, None] * ROW_DEV + (jnp.arange(ROW_DEV * TOP, dtype=jnp.int32) // TOP)[None, :]).astype(jnp.int32)
    source = jnp.broadcast_to(jnp.arange(owners, dtype=jnp.int32)[:, None], slots.shape)
    table = jnp.full((owners, COARSE * MOST), -1, jnp.int32).at[source, slots].set(pair_row)
    orders = jnp.argsort(local[parent.reshape(owners, block_size)], axis=1, stable=True).astype(jnp.int32)
    prior = float(PRIOR)
    fine = fine_cent.reshape(owners, block_size, D)
    coarse = coarse_cent
    for turn in range(ITERS):
        weights = coarse_weights(rows, coarse_ids, coarse)
        wire = weights.astype(jnp.bfloat16).reshape(owners, ROW_DEV * TOP)
        qtable = jnp.zeros((owners, COARSE * MOST), jnp.bfloat16).at[source, slots].set(wire)

        def one_owner(index):
            slot_rows = lax.dynamic_slice_in_dim(table, index * width, width, 1)
            slot_q = lax.dynamic_slice_in_dim(qtable, index * width, width, 1)
            gathered = rows[jnp.maximum(slot_rows, 0)]
            arrived = jnp.where((slot_rows >= 0)[..., None], gathered, jnp.zeros_like(gathered))
            order = orders[index]
            sorted_cent = fine[index][order].reshape(per_owner, CHILD, D)
            updated = owner_update(arrived.reshape(owners, per_owner, MOST, D), slot_q.reshape(owners, per_owner, MOST), sorted_cent)
            return jnp.zeros((block_size, D), jnp.bfloat16).at[order].set(updated.reshape(block_size, D))
        new_fine = lax.map(one_owner, jnp.arange(owners, dtype=jnp.int32))
        coarse = coarse_update(rows, coarse_ids, weights, coarse, prior)
        fine = new_fine
    return (fine.reshape(FINE, D), coarse)
```

```python
import functools
import math

import jax
import jax.numpy as jnp
from jax import lax
from jax.experimental import pallas as pl
from jax.experimental.pallas import tpu as pltpu
from jax.sharding import PartitionSpec as P

ITERS = 2
MOST = 4
BF = jnp.bfloat16
F32 = jnp.float32
NT = (((1,), (1,)), ((), ()))
TN = (((0,), (0,)), ((), ()))


def gather_kernel(nz, nc, rows_ref, ids_ref, rows_all, ids_all, rsend, rrecv, isend, irecv, local_sem):
    nx = nc // 2
    g = lax.axis_index("groups")
    z = lax.axis_index("dp")
    ce = lax.axis_index("cent")
    x = ce // 2
    core = ce % 2
    other = x * 2 + (1 - core)
    here = lambda zz, cc: (g, zz, cc)

    barrier = pltpu.get_barrier_semaphore()
    links = [
        (z > 0, here(z - 1, ce)),
        (z < nz - 1, here(z + 1, ce)),
        (x > 0, here(z, ce - 2)),
        (x < nx - 1, here(z, ce + 2)),
    ]
    for ok, dev in links:
        @pl.when(ok)
        def _():
            pl.semaphore_signal(barrier, inc=1, device_id=dev, device_id_type=pl.DeviceIdType.MESH)
    pl.semaphore_signal(
        barrier, inc=1, device_id=here(z, other), device_id_type=pl.DeviceIdType.MESH
    )
    mine = pltpu.make_async_copy(rows_ref, rows_all.at[z, ce], local_sem)
    mine.start()
    ids_all[z, ce] = ids_ref[...]
    degree = 1 + sum(ok.astype(jnp.int32) for ok, _ in links)
    mine.wait()
    pl.semaphore_wait(barrier, degree)

    def copies(zc, cc, way, dev):
        out = []
        for buf, ss, rs in ((rows_all, rsend, rrecv), (ids_all, isend, irecv)):
            out.append(
                pltpu.make_async_remote_copy(
                    src_ref=buf.at[zc, cc],
                    dst_ref=buf.at[zc, cc],
                    send_sem=ss.at[way, zc, cc],
                    recv_sem=rs.at[zc, cc],
                    device_id=dev,
                    device_id_type=pl.DeviceIdType.MESH,
                )
            )
        return out

    def send(zc, cc, way, dev, ok=None):
        def go():
            for c in copies(zc, cc, way, dev):
                c.start()
        if ok is None:
            go()
        else:
            pl.when(ok)(go)

    def wait_in(zc, cc):
        for c in copies(zc, cc, 0, here(z, other)):
            c.wait_recv()

    def on_x(zc, xc, right, left):
        cc = xc * 2 + core
        send(zc, cc, 3, here(z, ce + 2), right & (x < nx - 1))
        send(zc, cc, 2, here(z, ce - 2), left & (x > 0))
        send(zc, cc, 4, here(z, other))

    true = z >= 0

    def z_chunk(zc, up, down):
        send(zc, ce, 1, here(z + 1, ce), up & (z < nz - 1))
        send(zc, ce, 0, here(z - 1, ce), down & (z > 0))
        on_x(zc, x, true, true)

    def each_z(d, fn):
        if d == 0:
            fn(z, 0)
            return
        for sign in (-1, 1):
            zc = z + sign * d
            @pl.when((zc >= 0) & (zc < nz))
            def _():
                fn(zc, sign)

    def z_step(zc, sign):
        if sign == 0:
            z_chunk(zc, true, true)
        else:
            wait_in(zc, ce)
            z_chunk(zc, true if sign < 0 else ~true, true if sign > 0 else ~true)

    for t in range(nz + nx - 1):
        if t < nz:
            each_z(t, z_step)
        for e in range(1, nx):
            d = t - e
            if d < 0 or d >= nz:
                continue
            for sign in (-1, 1):
                xc = x + sign * e
                @pl.when((xc >= 0) & (xc < nx))
                def _():
                    def one(zc, _):
                        wait_in(zc, xc * 2 + core)
                        on_x(zc, xc, true if sign < 0 else ~true, true if sign > 0 else ~true)
                    each_z(d, one)

    for t in range(nz):
        def one(zc, _):
            for xc in range(nx):
                wait_in(zc, xc * 2 + (1 - core))
        each_z(t, one)
    def sent(zc, cc, way, ok):
        @pl.when(ok)
        def _():
            for c in copies(zc, cc, way, here(z, other)):
                c.wait_send()
    for zc in range(nz):
        sent(zc, ce, 1, (zc <= z) & (z < nz - 1))
        sent(zc, ce, 0, (zc >= z) & (z > 0))
        for xc in range(nx):
            cc = xc * 2 + core
            sent(zc, cc, 3, (xc <= x) & (x < nx - 1))
            sent(zc, cc, 2, (xc >= x) & (x > 0))
            sent(zc, cc, 4, true)


def gather(nz, nc, rows, ids):
    count, width = rows.shape
    return pl.pallas_call(
        functools.partial(gather_kernel, nz, nc),
        out_shape=(
            jax.ShapeDtypeStruct((nz, nc, count, width), BF),
            jax.ShapeDtypeStruct((nz, nc) + ids.shape, jnp.int32),
        ),
        in_specs=[pl.BlockSpec(memory_space=pltpu.VMEM)] * 2,
        out_specs=(pl.BlockSpec(memory_space=pltpu.VMEM),) * 2,
        scratch_shapes=[
            pltpu.SemaphoreType.DMA((5, nz, nc)),
            pltpu.SemaphoreType.DMA((nz, nc)),
            pltpu.SemaphoreType.DMA((5, nz, nc)),
            pltpu.SemaphoreType.DMA((nz, nc)),
            pltpu.SemaphoreType.DMA,
        ],
        compiler_params=pltpu.CompilerParams(
            collective_id=0, has_side_effects=True, vmem_limit_bytes=40 * 2**20
        ),
    )(rows, ids)


def iota(shape, dim):
    return lax.broadcasted_iota(jnp.int32, shape, dim)


def update_kernel(
    senders, per_sender, owned, rows_ref, ids_ref, parent_ref, fine_ref, coarse_ref,
    fine_out, coarse_out, match, mrank, qbuf, arrived, logit, cent, parent_col, sel,
):
    total, width = rows_ref.shape
    coarse_n = coarse_ref.shape[0]
    block = fine_ref.shape[0]
    slot_w = owned * MOST
    slots = senders * slot_w
    scale = 1.0 / math.sqrt(width)
    log2e = math.log2(math.e)
    prior = float(max(1, total // coarse_n))
    per_group = max(1, 128 // slot_w)
    group_rows = per_group * per_sender
    group_slots = per_group * slot_w
    groups = senders // per_group
    tile = min(512, block)
    tiles = block // tile

    nz_rows = block // 128
    me = lax.axis_index("dp") * lax.axis_size("cent") + lax.axis_index("cent")
    own = parent_ref[pl.ds(pl.multiple_of(me * nz_rows, nz_rows), nz_rows), :]
    if nz_rows < 8:
        own = jnp.concatenate([own] * (8 // nz_rows), axis=0)
    own_t = jnp.transpose(own.astype(F32))
    present = jnp.zeros((128, coarse_n), jnp.bool_)
    lanes = iota((128, coarse_n), 1)
    for b in range(nz_rows):
        col = own_t[:, b : b + 1].astype(jnp.int32)
        parent_col[pl.ds(b * 128, 128), :] = jnp.broadcast_to(col, (128, 128))
        present = present | (col == lanes)
    present_row = jnp.max(present.astype(F32), axis=0, keepdims=True)
    ci = iota((coarse_n, coarse_n), 0)
    cj = iota((coarse_n, coarse_n), 1)
    local_col = jnp.sum(jnp.where(cj < ci, present_row, 0.0), axis=1, keepdims=True)
    present_col = jnp.sum(jnp.where(cj == ci, present_row, 0.0), axis=1, keepdims=True)
    slot_i = iota((coarse_n, group_slots), 1)
    slot_local = (slot_i % slot_w // MOST).astype(F32)
    e_hit = (local_col == slot_local) & (present_col > 0.5)
    e_mat = e_hit.astype(BF)
    slot_cluster = jnp.sum(
        jnp.where(e_hit, iota((coarse_n, group_slots), 0), 0), axis=0, keepdims=True
    )
    slot_cluster = jnp.concatenate([slot_cluster] * groups, axis=1)

    ids_t = jnp.transpose(ids_ref[...].astype(F32))
    kk = ids_ref.shape[0] // senders
    row_lane = iota((per_sender, coarse_n), 1).astype(F32)
    for s in range(senders):
        hit = jnp.zeros((per_sender, coarse_n), jnp.bool_)
        for k in range(MOST):
            hit = hit | (ids_t[:per_sender, s * kk + k : s * kk + k + 1] == row_lane)
        match[pl.ds(s * per_sender, per_sender), :] = hit.astype(F32)
    step = 256
    ri = iota((step, step), 0)
    rj = iota((step, step), 1)
    lower = ((rj <= ri) & (rj // per_sender == ri // per_sender)).astype(BF)
    for b in range(total // step):
        m = match[pl.ds(b * step, step), :]
        upto = jnp.dot(lower, m.astype(BF), preferred_element_type=F32)
        mrank[pl.ds(b * step, step), :] = (upto * m).astype(BF)
    want = (iota((group_rows, group_slots), 1) % MOST + 1).astype(F32)
    same = (
        iota((group_rows, group_slots), 0) // per_sender
        == iota((group_rows, group_slots), 1) // slot_w
    )
    for b in range(groups):
        part = pl.ds(b * group_rows, group_rows)
        rank_e = jnp.dot(mrank[part, :], e_mat, preferred_element_type=F32)
        pick = (rank_e == want) & same
        sel[part, :] = pick.astype(BF)
        arrived[pl.ds(b * group_slots, group_slots), :] = lax.dot_general(
            pick.astype(BF), rows_ref[part, :], TN, preferred_element_type=F32
        ).astype(BF)

    ones = jnp.ones((total, 128), BF)
    for turn in range(ITERS):
        c_ref = coarse_ref if turn == 0 else coarse_out
        f_ref = fine_ref if turn == 0 else cent
        to_ref = fine_out if turn == ITERS - 1 else cent
        cf = c_ref[...].astype(F32)
        half = 0.5 * jnp.sum(cf * cf, axis=1, keepdims=True)
        half_row = jnp.sum(jnp.where(ci == cj, half, 0.0), axis=0, keepdims=True)
        dots = lax.dot_general(rows_ref[...], c_ref[...], NT, preferred_element_type=F32)
        masked = jnp.where(match[...] > 0.5, (dots - half_row) * scale, -jnp.inf)
        top = jnp.max(masked, axis=1, keepdims=True)
        ex = jnp.exp(masked - top)
        qb = (ex / jnp.sum(ex, axis=1, keepdims=True)).astype(BF)
        qbuf[...] = qb
        csum = lax.dot_general(qb, rows_ref[...], TN, preferred_element_type=F32)
        cmass = lax.dot_general(qb, ones, TN, preferred_element_type=F32)[:, :1]
        coarse_out[...] = ((csum + prior * cf) / (cmass + prior)).astype(BF)

        slot_q = []
        for b in range(groups):
            part = pl.ds(b * group_rows, group_rows)
            qe = jnp.dot(qbuf[part, :], e_mat, preferred_element_type=F32)
            slot_q.append(
                jnp.sum(qe * sel[part, :].astype(F32), axis=0, keepdims=True)
            )
        slot_q = jnp.concatenate(slot_q, axis=1)

        best = jnp.full((1, slots), -jnp.inf, F32)
        for b in range(tiles):
            part = pl.ds(b * tile, tile)
            ft = f_ref[part, :]
            ff = ft.astype(F32)
            norm = 0.5 * jnp.sum(ff * ff, axis=1, keepdims=True)
            d = lax.dot_general(ft, arrived[...], NT, preferred_element_type=F32)
            allowed = parent_col[part, :1] == slot_cluster
            l = jnp.where(allowed, (d - norm) * (scale * log2e), -jnp.inf)
            logit[part, :] = l
            best = jnp.maximum(best, jnp.max(l, axis=0, keepdims=True))
        denom = jnp.zeros((1, slots), F32)
        for b in range(tiles):
            part = pl.ds(b * tile, tile)
            e = jnp.exp2(logit[part, :] - best)
            logit[part, :] = e
            denom = denom + jnp.sum(e, axis=0, keepdims=True)
        factor = slot_q / denom
        for b in range(tiles):
            part = pl.ds(b * tile, tile)
            resp = logit[part, :] * factor
            mass = jnp.sum(resp, axis=1, keepdims=True)
            fsum = jnp.dot(resp.astype(BF), arrived[...], preferred_element_type=F32)
            to_ref[part, :] = (
                (fsum + f_ref[part, :].astype(F32)) * (1.0 / (mass + 1.0))
            ).astype(BF)


def update(senders, per_sender, rows, ids, parent, fine, coarse):
    total, width = rows.shape
    coarse_n = coarse.shape[0]
    block = fine.shape[0]
    owned = coarse_n // senders
    slots = senders * owned * MOST
    group_slots = max(1, 128 // (owned * MOST)) * owned * MOST
    return pl.pallas_call(
        functools.partial(update_kernel, senders, per_sender, owned),
        out_shape=(
            jax.ShapeDtypeStruct(fine.shape, BF),
            jax.ShapeDtypeStruct(coarse.shape, BF),
        ),
        in_specs=[pl.BlockSpec(memory_space=pltpu.VMEM)] * 5,
        out_specs=(pl.BlockSpec(memory_space=pltpu.VMEM),) * 2,
        scratch_shapes=[
            pltpu.VMEM((total, coarse_n), F32),
            pltpu.VMEM((total, coarse_n), BF),
            pltpu.VMEM((total, coarse_n), BF),
            pltpu.VMEM((slots, width), BF),
            pltpu.VMEM((block, slots), F32),
            pltpu.VMEM((block, width), BF),
            pltpu.VMEM((block, 128), jnp.int32),
            pltpu.VMEM((total, group_slots), BF),
        ],
        compiler_params=pltpu.CompilerParams(vmem_limit_bytes=56 * 2**20),
    )(rows, ids, parent, fine, coarse)


def on_device(rows, coarse_ids, parent, fine_cent, coarse_cent):
    nz = lax.axis_size("dp")
    nc = lax.axis_size("cent")
    senders = nz * nc
    per_sender, width = rows.shape
    ids = jnp.pad(
        coarse_ids.T, ((0, 8 - coarse_ids.shape[1]), (0, 128 - per_sender)), constant_values=-1
    )
    rows_all, ids_all = gather(nz, nc, rows, ids)
    return update(
        senders,
        per_sender,
        rows_all.reshape(senders * per_sender, width),
        ids_all.reshape(senders * 8, 128),
        parent.reshape(-1, 128),
        fine_cent,
        coarse_cent,
    )


def solution(mesh):
    in_specs = (
        P(("groups", "dp", "cent"), None),
        P(("groups", "dp", "cent"), None),
        P("groups"),
        P(("groups", "dp", "cent"), None),
        P("groups", None),
    )
    out_specs = (P(("groups", "dp", "cent"), None), P("groups", None))
    return jax.shard_map(
        on_device, mesh=mesh, in_specs=in_specs, out_specs=out_specs, check_vma=False
    )
```

```python
import functools
import math

import jax
import jax.numpy as jnp
from jax import lax
from jax.experimental import pallas as pl
from jax.experimental.pallas import tpu as pltpu
from jax.sharding import PartitionSpec as P

ITERS = 2
MOST = 4
VMEM_LIMIT = 60 * 2**20
BF = jnp.bfloat16
F32 = jnp.float32
NT = (((1,), (1,)), ((), ()))
TN = (((0,), (0,)), ((), ()))


def iota(shape, dim):
    return lax.broadcasted_iota(jnp.int32, shape, dim)


def first_kernel(
    nz, nc, owned, rows_ref, ids_hbm, parent_hbm, fine_hbm, coarse_hbm,
    f1_out, arrived_out, pcol_out, scl_hbm, sq_hbm, c2_hbm,
    arrived, pcol, scl_out, sq_out, c2_out,
    rows_all, ids_all, match, sel, norms, logit, facc, masses, csum, cmass, c1, sq_first,
    ids_ref, parent_ref, fine_ref, coarse_ref,
    rsend, rrecv, isend, irecv, local_sem, out_sem,
):
    per_sender, width = rows_ref.shape
    senders = nz * nc
    total = senders * per_sender
    coarse_n = coarse_ref.shape[0]
    block = fine_ref.shape[0]
    tops = ids_hbm.shape[0]
    slot_w = owned * MOST
    scale = 1.0 / math.sqrt(width)
    scale2 = scale * math.log2(math.e)
    prior = float(max(1, total // coarse_n))
    per_group = 128 // slot_w
    planes = per_group // nc
    group_rows = per_group * per_sender
    groups = senders // per_group
    tile = min(512, block)
    tiles = block // tile
    parts = [pl.ds(b * tile, tile) for b in range(tiles)]
    interleave = planes == 1

    nx = nc // 2
    g = lax.axis_index("groups")
    z = lax.axis_index("dp")
    ce = lax.axis_index("cent")
    x = ce // 2
    core = ce % 2
    other = x * 2 + (1 - core)
    here = lambda zz, cc: (g, zz, cc)

    barrier = pltpu.get_barrier_semaphore()
    links = [
        (z > 0, here(z - 1, ce)),
        (z < nz - 1, here(z + 1, ce)),
        (x > 0, here(z, ce - 2)),
        (x < nx - 1, here(z, ce + 2)),
    ]
    for ok, dev in links:
        @pl.when(ok)
        def _():
            pl.semaphore_signal(barrier, inc=1, device_id=dev, device_id_type=pl.DeviceIdType.MESH)
    pl.semaphore_signal(
        barrier, inc=1, device_id=here(z, other), device_id_type=pl.DeviceIdType.MESH
    )
    loads = [
        pltpu.make_async_copy(a, b, local_sem.at[i])
        for i, (a, b) in enumerate(
            [
                (rows_ref, rows_all.at[z, ce]),
                (ids_hbm, ids_ref),
                (coarse_hbm, coarse_ref),
                (parent_hbm, parent_ref),
                (fine_hbm, fine_ref),
            ]
        )
    ]
    for load in loads:
        load.start()
    degree = 1 + sum(ok.astype(jnp.int32) for ok, _ in links)
    loads[1].wait()
    ids_all[z, ce] = jnp.full((8, 128), -1, jnp.int32)
    ids_all[z, ce, :tops, :per_sender] = ids_ref[...]
    loads[0].wait()
    pl.semaphore_wait(barrier, degree)

    def copies(zc, cc, way, dev):
        out = []
        for buf, ss, rs in ((rows_all, rsend, rrecv), (ids_all, isend, irecv)):
            out.append(
                pltpu.make_async_remote_copy(
                    src_ref=buf.at[zc, cc],
                    dst_ref=buf.at[zc, cc],
                    send_sem=ss.at[way, zc, cc],
                    recv_sem=rs.at[zc, cc],
                    device_id=dev,
                    device_id_type=pl.DeviceIdType.MESH,
                )
            )
        return out

    def send(zc, cc, way, dev, ok=None):
        def go():
            for c in copies(zc, cc, way, dev):
                c.start()
        if ok is None:
            go()
        else:
            pl.when(ok)(go)

    def wait_in(zc, cc):
        for c in copies(zc, cc, 0, here(z, other)):
            c.wait_recv()

    def on_x(zc, xc, right, left):
        cc = xc * 2 + core
        send(zc, cc, 3, here(z, ce + 2), right & (x < nx - 1))
        send(zc, cc, 2, here(z, ce - 2), left & (x > 0))
        send(zc, cc, 4, here(z, other))

    true = z >= 0

    def z_chunk(zc, up, down):
        send(zc, ce, 1, here(z + 1, ce), up & (z < nz - 1))
        send(zc, ce, 0, here(z - 1, ce), down & (z > 0))
        on_x(zc, x, true, true)

    def each_z(d, fn):
        if d == 0:
            fn(z, 0)
            return
        for sign in (-1, 1):
            zc = z + sign * d
            @pl.when((zc >= 0) & (zc < nz))
            def _():
                fn(zc, sign)

    def z_step(zc, sign):
        if sign == 0:
            z_chunk(zc, true, true)
        else:
            wait_in(zc, ce)
            z_chunk(zc, true if sign < 0 else ~true, true if sign > 0 else ~true)

    def comm_step(t):
        if t < nz:
            each_z(t, z_step)
        for e in range(1, nx):
            d = t - e
            if d < 0 or d >= nz:
                continue
            for sign in (-1, 1):
                xc = x + sign * e
                @pl.when((xc >= 0) & (xc < nx))
                def _():
                    def one(zc, _):
                        wait_in(zc, xc * 2 + core)
                        on_x(zc, xc, true if sign < 0 else ~true, true if sign > 0 else ~true)
                    each_z(d, one)

    def wait_other(zc):
        for xc in range(nx):
            wait_in(zc, xc * 2 + (1 - core))

    comm_step(0)

    loads[3].wait()
    own_rows = block // 128
    me = z * nc + ce
    own = parent_ref[pl.ds(pl.multiple_of(me * own_rows, own_rows), own_rows), :]
    if own_rows < 8:
        own = jnp.concatenate([own] * (8 // own_rows), axis=0)
    own_t = jnp.transpose(own.astype(F32))
    present = jnp.zeros((128, coarse_n), jnp.bool_)
    lanes = iota((128, coarse_n), 1)
    for b in range(own_rows):
        col = own_t[:, b : b + 1].astype(jnp.int32)
        pcol[pl.ds(b * 128, 128), :] = jnp.broadcast_to(col, (128, 128))
        present = present | (col == lanes)
    present_row = jnp.max(present.astype(F32), axis=0, keepdims=True)
    ci = iota((coarse_n, coarse_n), 0)
    cj = iota((coarse_n, coarse_n), 1)
    local_col = jnp.sum(jnp.where(cj < ci, present_row, 0.0), axis=1, keepdims=True)
    present_col = jnp.sum(jnp.where(cj == ci, present_row, 0.0), axis=1, keepdims=True)
    slot_local = (iota((coarse_n, 128), 1) % slot_w // MOST).astype(F32)
    e_hit = (local_col == slot_local) & (present_col > 0.5)
    e_mat = e_hit.astype(BF)
    slot_cluster = jnp.sum(jnp.where(e_hit, iota((coarse_n, 128), 0), 0), axis=0, keepdims=True)
    scl_out[...] = jnp.broadcast_to(slot_cluster, (8, 128))
    outs = [pltpu.make_async_copy(pcol, pcol_out, out_sem.at[0])]
    outs[0].start()
    outs.append(pltpu.make_async_copy(scl_out, scl_hbm, out_sem.at[1]))
    outs[1].start()
    step = 256
    ri = iota((step, step), 0)
    rj = iota((step, step), 1)
    lower = ((rj <= ri) & (rj // per_sender == ri // per_sender)).astype(BF)
    want = (iota((group_rows, 128), 1) % MOST + 1).astype(F32)
    same = iota((group_rows, 128), 0) // per_sender == iota((group_rows, 128), 1) // slot_w
    row_lane = iota((per_sender, coarse_n), 1).astype(F32)
    ones = jnp.ones((group_rows, 128), BF)

    def half_row_of(c_ref):
        cf = c_ref[...].astype(F32)
        half = 0.5 * jnp.sum(cf * cf, axis=1, keepdims=True)
        return jnp.sum(jnp.where(ci == cj, half, 0.0), axis=0, keepdims=True)

    def rows_of(b):
        return rows_all[pl.ds(b * planes, planes)].reshape(group_rows, width)

    def span(b, size):
        return pl.ds(pl.multiple_of(b * size, size), size)

    def coarse_group(b, rows_g, c_ref, half_row, hit):
        dots = lax.dot_general(rows_g, c_ref[...], NT, preferred_element_type=F32)
        masked = jnp.where(hit > 0.5, (dots - half_row) * scale, -jnp.inf)
        top = jnp.max(masked, axis=1, keepdims=True)
        ex = jnp.exp(masked - top)
        qb = (ex / jnp.sum(ex, axis=1, keepdims=True)).astype(BF)
        csum[...] += lax.dot_general(qb, rows_g, TN, preferred_element_type=F32)
        cmass[...] += lax.dot_general(qb, ones, TN, preferred_element_type=F32)
        qe = jnp.dot(qb, e_mat, preferred_element_type=F32)
        return jnp.sum(
            qe * sel[span(b, group_rows), :].astype(F32), axis=0, keepdims=True
        )

    def coarse_end(c_ref, to_ref):
        to_ref[...] = (
            (csum[...] + prior * c_ref[...].astype(F32)) / (cmass[:, :1] + prior)
        ).astype(BF)

    loads[2].wait()
    half_first = half_row_of(coarse_ref)
    csum[...] = jnp.zeros_like(csum)
    cmass[...] = jnp.zeros_like(cmass)

    def prep(b):
        rows_g = rows_of(b)
        ids_t = jnp.transpose(
            ids_all[pl.ds(b * planes, planes)].reshape(per_group * 8, 128).astype(F32)
        )
        hits = []
        for s in range(per_group):
            hit = jnp.zeros((per_sender, coarse_n), jnp.bool_)
            for k in range(MOST):
                hit = hit | (ids_t[:per_sender, s * 8 + k : s * 8 + k + 1] == row_lane)
            hits.append(hit.astype(F32))
        hit = jnp.concatenate(hits, axis=0)
        match[span(b, group_rows), :] = hit
        ranks = []
        for i in range(group_rows // step):
            m = hit[i * step : (i + 1) * step]
            upto = jnp.dot(lower, m.astype(BF), preferred_element_type=F32)
            ranks.append((upto * m).astype(BF))
        rank = jnp.concatenate(ranks, axis=0)
        rank_e = jnp.dot(rank, e_mat, preferred_element_type=F32)
        pick = ((rank_e == want) & same).astype(BF)
        sel[span(b, group_rows), :] = pick
        slots_g = lax.dot_general(pick, rows_g, TN, preferred_element_type=F32).astype(BF)
        arrived[span(b, 128), :] = slots_g
        slot_q = coarse_group(b, rows_g, coarse_ref, half_first, hit)
        sq_first[b] = jnp.broadcast_to(slot_q, (8, 128))

    cluster2 = jnp.concatenate([slot_cluster] * 2, axis=1)
    twice = lambda v: jnp.concatenate([v, v], axis=1)

    def pair_slots(b0, b1):
        return jnp.concatenate([arrived[span(b0, 128), :], arrived[span(b1, 128), :]], axis=0)

    def pair_prob(b0, b1):
        slots_g = pair_slots(b0, b1)
        best = jnp.full((1, 256), -jnp.inf, F32)
        for part in parts:
            d = lax.dot_general(fine_ref[part, :], slots_g, NT, preferred_element_type=F32)
            l = jnp.where(
                twice(pcol[part, :]) == cluster2, (d - twice(norms[part, :])) * scale2, -jnp.inf
            )
            logit[part, :] = l
            best = jnp.maximum(best, jnp.max(l, axis=0, keepdims=True))
        denom = jnp.zeros((1, 256), F32)
        for part in parts:
            e = jnp.exp2(logit[part, :] - best)
            logit[part, :] = e
            denom = denom + jnp.sum(e, axis=0, keepdims=True)
        return jnp.concatenate([sq_first[b0][:1], sq_first[b1][:1]], axis=1) / denom

    def pair_sum(i, b0, b1, factor):
        slots_g = pair_slots(b0, b1)
        for part in parts:
            resp = logit[part, :] * factor
            fsum = jnp.dot(resp.astype(BF), slots_g, preferred_element_type=F32)
            mass = resp[:, :128] + resp[:, 128:]
            if i > 0:
                fsum = fsum + facc[part, :]
                mass = mass + masses[part, :]
            if i < groups // 2 - 1:
                facc[part, :] = fsum
                masses[part, :] = mass
            else:
                fine_ref[part, :] = (
                    (fsum + fine_ref[part, :].astype(F32))
                    * (1.0 / (jnp.sum(mass, axis=1, keepdims=True) + 1.0))
                ).astype(BF)
                outs.append(
                    pltpu.make_async_copy(
                        fine_ref.at[part, :], f1_out.at[part, :], out_sem.at[len(outs)]
                    )
                )
                outs[-1].start()

    def arrived_copy():
        outs.append(pltpu.make_async_copy(arrived, arrived_out, out_sem.at[len(outs)]))
        outs[-1].start()

    def fill_norms():
        loads[4].wait()
        for part in parts:
            ff = fine_ref[part, :].astype(F32)
            half = 0.5 * jnp.sum(ff * ff, axis=1, keepdims=True)
            norms[part, :] = jnp.broadcast_to(half, (tile, 128))

    last = nz + nx - 1
    if interleave:
        up = z < nz // 2
        order = [jnp.where(up, (z + k) % nz, (z - k + nz) % nz) for k in range(nz)]
        pairs = [(order[2 * i], order[2 * i + 1]) for i in range(nz // 2)]
        for t in range(1, last):
            comm_step(t)
            k = t - (nx - 1)
            if k == 0:
                fill_norms()
            if 0 <= k < nz // 2:
                wait_other(order[k])
                prep(order[k])
            elif k == nz // 2:
                pair_sum(0, *pairs[0], pair_prob(*pairs[0]))
        for k in range(nz // 2, nz):
            wait_other(order[k])
            prep(order[k])
        arrived_copy()
        for i in range(1, nz // 2):
            pair_sum(i, *pairs[i], pair_prob(*pairs[i]))
    else:
        fill_norms()
        for t in range(1, last):
            comm_step(t)
        for t in range(nz):
            each_z(t, lambda zc, _: wait_other(zc))
        lax.fori_loop(0, groups, lambda b, c: (prep(b), c)[1], 0)
        arrived_copy()
        for i in range(groups // 2):
            pair_sum(i, 2 * i, 2 * i + 1, pair_prob(2 * i, 2 * i + 1))

    coarse_end(coarse_ref, c1)
    half_second = half_row_of(c1)
    csum[...] = jnp.zeros_like(csum)
    cmass[...] = jnp.zeros_like(cmass)

    def second(b):
        slot_q = coarse_group(b, rows_of(b), c1, half_second, match[span(b, group_rows), :])
        sq_out[b] = jnp.broadcast_to(slot_q, (8, 128))

    if interleave:
        rows_g = rows_all[...].reshape(total, width)
        dots = lax.dot_general(rows_g, c1[...], NT, preferred_element_type=F32)
        masked = jnp.where(match[...] > 0.5, (dots - half_second) * scale, -jnp.inf)
        ex = jnp.exp(masked - jnp.max(masked, axis=1, keepdims=True))
        qb = (ex * (1.0 / jnp.sum(ex, axis=1, keepdims=True))).astype(BF)
        csum[...] = lax.dot_general(qb, rows_g, TN, preferred_element_type=F32)
        mass_row = jnp.sum(qb.astype(F32), axis=0, keepdims=True)
        mass_col = jnp.sum(jnp.where(ci == cj, mass_row, 0.0), axis=1, keepdims=True)
        cmass[...] = jnp.broadcast_to(mass_col, cmass.shape)
        qe = jnp.dot(qb, e_mat, preferred_element_type=F32) * sel[...].astype(F32)
        for b in range(groups):
            slot_q = jnp.sum(
                qe[b * group_rows : (b + 1) * group_rows], axis=0, keepdims=True
            )
            sq_out[b] = jnp.broadcast_to(slot_q, (8, 128))
    else:
        lax.fori_loop(0, groups, lambda b, c: (second(b), c)[1], 0)
    coarse_end(c1, c2_out)

    for src, dst in ((sq_out, sq_hbm), (c2_out, c2_hbm)):
        outs.append(pltpu.make_async_copy(src, dst, out_sem.at[len(outs)]))
        outs[-1].start()
    for c in outs:
        c.wait()
    def sent(zc, cc, way, ok):
        @pl.when(ok)
        def _():
            for c in copies(zc, cc, way, here(z, other)):
                c.wait_send()
    for zc in range(nz):
        sent(zc, ce, 1, (zc <= z) & (z < nz - 1))
        sent(zc, ce, 0, (zc >= z) & (z > 0))
        for xc in range(nx):
            cc = xc * 2 + core
            sent(zc, cc, 3, (xc <= x) & (x < nx - 1))
            sent(zc, cc, 2, (xc >= x) & (x > 0))
            sent(zc, cc, 4, true)


def first(nz, nc, rows, ids, parent, fine, coarse):
    per_sender, width = rows.shape
    senders = nz * nc
    total = senders * per_sender
    coarse_n = coarse.shape[0]
    block = fine.shape[0]
    owned = coarse_n // senders
    slots = senders * owned * MOST
    groups = slots // 128
    return pl.pallas_call(
        functools.partial(first_kernel, nz, nc, owned),
        out_shape=(
            jax.ShapeDtypeStruct(fine.shape, BF),
            jax.ShapeDtypeStruct((slots, width), BF),
            jax.ShapeDtypeStruct((block, 128), jnp.int32),
            jax.ShapeDtypeStruct((8, 128), jnp.int32),
            jax.ShapeDtypeStruct((groups, 8, 128), F32),
            jax.ShapeDtypeStruct(coarse.shape, BF),
        ),
        in_specs=[pl.BlockSpec(memory_space=pltpu.HBM)] * 5,
        out_specs=(pl.BlockSpec(memory_space=pltpu.HBM),) * 6,
        scratch_shapes=[
            pltpu.VMEM((slots, width), BF),
            pltpu.VMEM((block, 128), jnp.int32),
            pltpu.VMEM((8, 128), jnp.int32),
            pltpu.VMEM((groups, 8, 128), F32),
            pltpu.VMEM(coarse.shape, BF),
            pltpu.VMEM((nz, nc) + rows.shape, BF),
            pltpu.VMEM((nz, nc, 8, 128), jnp.int32),
            pltpu.VMEM((total, coarse_n), F32),
            pltpu.VMEM((total, 128), BF),
            pltpu.VMEM((block, 128), F32),
            pltpu.VMEM((block, 256), F32),
            pltpu.VMEM(fine.shape, F32),
            pltpu.VMEM((block, 128), F32),
            pltpu.VMEM(coarse.shape, F32),
            pltpu.VMEM((coarse_n, 128), F32),
            pltpu.VMEM(coarse.shape, BF),
            pltpu.VMEM((groups, 8, 128), F32),
            pltpu.VMEM(ids.shape, jnp.int32),
            pltpu.VMEM(parent.shape, jnp.int32),
            pltpu.VMEM(fine.shape, BF),
            pltpu.VMEM(coarse.shape, BF),
            pltpu.SemaphoreType.DMA((5, nz, nc)),
            pltpu.SemaphoreType.DMA((nz, nc)),
            pltpu.SemaphoreType.DMA((5, nz, nc)),
            pltpu.SemaphoreType.DMA((nz, nc)),
            pltpu.SemaphoreType.DMA((5,)),
            pltpu.SemaphoreType.DMA((5 + max(1, block // 512),)),
        ],
        compiler_params=pltpu.CompilerParams(
            collective_id=0,
            has_side_effects=True,
            vmem_limit_bytes=VMEM_LIMIT,
        ),
    )(rows, ids, parent, fine, coarse)


def second_kernel(
    f1_hbm, arrived_hbm, pcol_hbm, scl_hbm, sq_hbm, c2_hbm, fine_out, coarse_out,
    scl_ref, sq_ref, logit, result, f1_ref, arrived, pcol, sems, in_sems,
):
    block, width = f1_hbm.shape
    groups = sq_hbm.shape[0]
    slots = groups * 128
    scale2 = math.log2(math.e) / math.sqrt(width)
    tile = min(512, block)
    parts = [pl.ds(b * tile, tile) for b in range(block // tile)]
    small = [
        pltpu.make_async_copy(a, b, in_sems.at[i])
        for i, (a, b) in enumerate(
            [(arrived_hbm, arrived), (scl_hbm, scl_ref), (sq_hbm, sq_ref), (c2_hbm, coarse_out)]
        )
    ]
    for c in small:
        c.start()
    loads = []
    for b, part in enumerate(parts):
        loads.append(
            [
                pltpu.make_async_copy(src.at[part, :], dst.at[part, :], in_sems.at[4 + 2 * b + i])
                for i, (src, dst) in enumerate([(f1_hbm, f1_ref), (pcol_hbm, pcol)])
            ]
        )
        for c in loads[-1]:
            c.start()
    for c in small[:3]:
        c.wait()
    slot_cluster = jnp.concatenate([scl_ref[:1, :]] * groups, axis=1)
    slot_q = jnp.concatenate([sq_ref[b, :1, :] for b in range(groups)], axis=1)
    best = jnp.full((1, slots), -jnp.inf, F32)
    for part, pending in zip(parts, loads):
        for c in pending:
            c.wait()
        ft = f1_ref[part, :]
        ff = ft.astype(F32)
        norm = 0.5 * jnp.sum(ff * ff, axis=1, keepdims=True)
        d = lax.dot_general(ft, arrived[...], NT, preferred_element_type=F32)
        same = jnp.concatenate([pcol[part, :]] * groups, axis=1) == slot_cluster
        l = jnp.where(same, (d - norm) * scale2, -jnp.inf)
        logit[part, :] = l
        best = jnp.maximum(best, jnp.max(l, axis=0, keepdims=True))
    denom = jnp.zeros((1, slots), F32)
    for part in parts:
        e = jnp.exp2(logit[part, :] - best)
        logit[part, :] = e
        denom = denom + jnp.sum(e, axis=0, keepdims=True)
    factor = slot_q / denom
    copies = [small[3]]
    for b, part in enumerate(parts):
        resp = logit[part, :] * factor
        mass = jnp.sum(resp, axis=1, keepdims=True)
        fsum = jnp.dot(resp.astype(BF), arrived[...], preferred_element_type=F32)
        result[part, :] = (
            (fsum + f1_ref[part, :].astype(F32)) * (1.0 / (mass + 1.0))
        ).astype(BF)
        copies.append(pltpu.make_async_copy(result.at[part, :], fine_out.at[part, :], sems.at[b]))
        copies[-1].start()
    for c in copies:
        c.wait()


def second(f1, arrived, pcol, scl, sq, c2):
    block, width = f1.shape
    slots = arrived.shape[0]
    return pl.pallas_call(
        second_kernel,
        out_shape=(jax.ShapeDtypeStruct(f1.shape, BF), jax.ShapeDtypeStruct(c2.shape, BF)),
        in_specs=[pl.BlockSpec(memory_space=pltpu.HBM)] * 6,
        out_specs=(pl.BlockSpec(memory_space=pltpu.HBM),) * 2,
        scratch_shapes=[
            pltpu.VMEM(scl.shape, jnp.int32),
            pltpu.VMEM(sq.shape, F32),
            pltpu.VMEM((block, slots), F32),
            pltpu.VMEM((block, width), BF),
            pltpu.VMEM((block, width), BF),
            pltpu.VMEM((slots, width), BF),
            pltpu.VMEM((block, 128), jnp.int32),
            pltpu.SemaphoreType.DMA((max(1, block // 512),)),
            pltpu.SemaphoreType.DMA((4 + 2 * max(1, block // 512),)),
        ],
        compiler_params=pltpu.CompilerParams(vmem_limit_bytes=VMEM_LIMIT),
    )(f1, arrived, pcol, scl, sq, c2)


def on_device(rows, coarse_ids, parent, fine_cent, coarse_cent):
    nz = lax.axis_size("dp")
    nc = lax.axis_size("cent")
    return second(*first(nz, nc, rows, coarse_ids.T, parent.reshape(-1, 128), fine_cent, coarse_cent))


def solution(mesh):
    in_specs = (
        P(("groups", "dp", "cent"), None),
        P(("groups", "dp", "cent"), None),
        P("groups"),
        P(("groups", "dp", "cent"), None),
        P("groups", None),
    )
    out_specs = (P(("groups", "dp", "cent"), None), P("groups", None))
    return jax.shard_map(
        on_device, mesh=mesh, in_specs=in_specs, out_specs=out_specs, check_vma=False
    )
```

```python
import functools
import math

import jax
import jax.numpy as jnp
from jax import lax
from jax.experimental import pallas as pl
from jax.experimental.pallas import tpu as pltpu
from jax.sharding import PartitionSpec as P

ITERS = 2
MOST = 4
VMEM_LIMIT = 60 * 2**20
FLOOR = -1e30


def tile_softmax(l):
    top = jnp.maximum(jnp.max(l, axis=0, keepdims=True), FLOOR)
    e = jnp.exp2(l - top)
    return e, top, jnp.sum(e, axis=0, keepdims=True)


def tile_factors(tops, sums, q):
    best = functools.reduce(jnp.maximum, tops)
    shares = [jnp.exp2(top - best) for top in tops]
    scale = q / sum(share * total for share, total in zip(shares, sums))
    return [share * scale for share in shares]
BF = jnp.bfloat16
F32 = jnp.float32
NT = (((1,), (1,)), ((), ()))
TN = (((0,), (0,)), ((), ()))


def iota(shape, dim):
    return lax.broadcasted_iota(jnp.int32, shape, dim)


def first_kernel(
    nz, nc, owned, rows_ref, ids_hbm, parent_hbm, fine_hbm, coarse_hbm,
    f1_out, arrived_out, pcol_out, scl_hbm, sq_hbm, c2_hbm,
    arrived, pcol, scl_out, sq_out, c2_out,
    rows_all, ids_all, match, sel, norms, logit, facc, masses, csum, cmass, c1, sq_first,
    ids_ref, parent_ref, fine_ref, coarse_ref,
    rsend, rrecv, isend, irecv, local_sem, out_sem,
):
    per_sender, width = rows_ref.shape
    senders = nz * nc
    total = senders * per_sender
    coarse_n = coarse_ref.shape[0]
    block = fine_ref.shape[0]
    tops = ids_hbm.shape[0]
    slot_w = owned * MOST
    scale = 1.0 / math.sqrt(width)
    scale2 = scale * math.log2(math.e)
    prior = float(max(1, total // coarse_n))
    per_group = 128 // slot_w
    planes = per_group // nc
    group_rows = per_group * per_sender
    groups = senders // per_group
    tile = min(512, block)
    tiles = block // tile
    parts = [pl.ds(b * tile, tile) for b in range(tiles)]
    interleave = planes == 1

    nx = nc // 2
    g = lax.axis_index("groups")
    z = lax.axis_index("dp")
    ce = lax.axis_index("cent")
    x = ce // 2
    core = ce % 2
    other = x * 2 + (1 - core)
    here = lambda zz, cc: (g, zz, cc)

    barrier = pltpu.get_barrier_semaphore()
    links = [
        (z > 0, here(z - 1, ce)),
        (z < nz - 1, here(z + 1, ce)),
        (x > 0, here(z, ce - 2)),
        (x < nx - 1, here(z, ce + 2)),
    ]
    for ok, dev in links:
        @pl.when(ok)
        def _():
            pl.semaphore_signal(barrier, inc=1, device_id=dev, device_id_type=pl.DeviceIdType.MESH)
    pl.semaphore_signal(
        barrier, inc=1, device_id=here(z, other), device_id_type=pl.DeviceIdType.MESH
    )
    loads = [
        pltpu.make_async_copy(a, b, local_sem.at[i])
        for i, (a, b) in enumerate(
            [
                (rows_ref, rows_all.at[z, ce]),
                (ids_hbm, ids_ref),
                (coarse_hbm, coarse_ref),
                (parent_hbm, parent_ref),
                (fine_hbm, fine_ref),
            ]
        )
    ]
    for load in loads:
        load.start()
    degree = 1 + sum(ok.astype(jnp.int32) for ok, _ in links)
    loads[1].wait()
    ids_all[z, ce] = jnp.full((8, 128), -1, jnp.int32)
    ids_all[z, ce, :tops, :per_sender] = ids_ref[...]
    loads[0].wait()
    pl.semaphore_wait(barrier, degree)

    def copies(zc, cc, way, dev):
        out = []
        for buf, ss, rs in ((rows_all, rsend, rrecv), (ids_all, isend, irecv)):
            out.append(
                pltpu.make_async_remote_copy(
                    src_ref=buf.at[zc, cc],
                    dst_ref=buf.at[zc, cc],
                    send_sem=ss.at[way, zc, cc],
                    recv_sem=rs.at[zc, cc],
                    device_id=dev,
                    device_id_type=pl.DeviceIdType.MESH,
                )
            )
        return out

    def send(zc, cc, way, dev, ok=None):
        def go():
            for c in copies(zc, cc, way, dev):
                c.start()
        if ok is None:
            go()
        else:
            pl.when(ok)(go)

    def wait_in(zc, cc):
        for c in copies(zc, cc, 0, here(z, other)):
            c.wait_recv()

    def on_x(zc, xc, right, left):
        cc = xc * 2 + core
        send(zc, cc, 3, here(z, ce + 2), right & (x < nx - 1))
        send(zc, cc, 2, here(z, ce - 2), left & (x > 0))
        send(zc, cc, 4, here(z, other))

    true = z >= 0

    def z_chunk(zc, up, down):
        send(zc, ce, 1, here(z + 1, ce), up & (z < nz - 1))
        send(zc, ce, 0, here(z - 1, ce), down & (z > 0))
        on_x(zc, x, true, true)

    def each_z(d, fn):
        if d == 0:
            fn(z, 0)
            return
        for sign in (-1, 1):
            zc = z + sign * d
            @pl.when((zc >= 0) & (zc < nz))
            def _():
                fn(zc, sign)

    def z_step(zc, sign):
        if sign == 0:
            z_chunk(zc, true, true)
        else:
            wait_in(zc, ce)
            z_chunk(zc, true if sign < 0 else ~true, true if sign > 0 else ~true)

    def comm_step(t):
        if t < nz:
            each_z(t, z_step)
        for e in range(1, nx):
            d = t - e
            if d < 0 or d >= nz:
                continue
            for sign in (-1, 1):
                xc = x + sign * e
                @pl.when((xc >= 0) & (xc < nx))
                def _():
                    def one(zc, _):
                        wait_in(zc, xc * 2 + core)
                        on_x(zc, xc, true if sign < 0 else ~true, true if sign > 0 else ~true)
                    each_z(d, one)

    def wait_other(zc):
        for xc in range(nx):
            wait_in(zc, xc * 2 + (1 - core))

    comm_step(0)

    loads[3].wait()
    own_rows = block // 128
    me = z * nc + ce
    own = parent_ref[pl.ds(pl.multiple_of(me * own_rows, own_rows), own_rows), :]
    if own_rows < 8:
        own = jnp.concatenate([own] * (8 // own_rows), axis=0)
    own_t = jnp.transpose(own.astype(F32))
    present = jnp.zeros((128, coarse_n), jnp.bool_)
    lanes = iota((128, coarse_n), 1)
    for b in range(own_rows):
        col = own_t[:, b : b + 1].astype(jnp.int32)
        pcol[pl.ds(b * 128, 128), :] = jnp.broadcast_to(col, (128, 128))
        present = present | (col == lanes)
    present_row = jnp.max(present.astype(F32), axis=0, keepdims=True)
    ci = iota((coarse_n, coarse_n), 0)
    cj = iota((coarse_n, coarse_n), 1)
    local_col = jnp.sum(jnp.where(cj < ci, present_row, 0.0), axis=1, keepdims=True)
    present_col = jnp.sum(jnp.where(cj == ci, present_row, 0.0), axis=1, keepdims=True)
    slot_local = (iota((coarse_n, 128), 1) % slot_w // MOST).astype(F32)
    e_hit = (local_col == slot_local) & (present_col > 0.5)
    e_mat = e_hit.astype(BF)
    slot_cluster = jnp.sum(jnp.where(e_hit, iota((coarse_n, 128), 0), 0), axis=0, keepdims=True)
    scl_out[...] = jnp.broadcast_to(slot_cluster, (8, 128))
    outs = [pltpu.make_async_copy(pcol, pcol_out, out_sem.at[0])]
    outs[0].start()
    outs.append(pltpu.make_async_copy(scl_out, scl_hbm, out_sem.at[1]))
    outs[1].start()
    step = 256
    ri = iota((step, step), 0)
    rj = iota((step, step), 1)
    lower = ((rj <= ri) & (rj // per_sender == ri // per_sender)).astype(BF)
    want = (iota((group_rows, 128), 1) % MOST + 1).astype(F32)
    same = iota((group_rows, 128), 0) // per_sender == iota((group_rows, 128), 1) // slot_w
    row_lane = iota((per_sender, coarse_n), 1).astype(F32)
    ones = jnp.ones((group_rows, 128), BF)

    def half_row_of(c_ref):
        cf = c_ref[...].astype(F32)
        half = 0.5 * jnp.sum(cf * cf, axis=1, keepdims=True)
        return jnp.sum(jnp.where(ci == cj, half, 0.0), axis=0, keepdims=True)

    def rows_of(b):
        return rows_all[pl.ds(b * planes, planes)].reshape(group_rows, width)

    def span(b, size):
        return pl.ds(pl.multiple_of(b * size, size), size)

    def coarse_group(b, rows_g, c_ref, half_row, hit):
        dots = lax.dot_general(rows_g, c_ref[...], NT, preferred_element_type=F32)
        masked = jnp.where(hit > 0.5, (dots - half_row) * scale, -jnp.inf)
        top = jnp.max(masked, axis=1, keepdims=True)
        ex = jnp.exp(masked - top)
        qb = (ex / jnp.sum(ex, axis=1, keepdims=True)).astype(BF)
        csum[...] += lax.dot_general(qb, rows_g, TN, preferred_element_type=F32)
        cmass[...] += lax.dot_general(qb, ones, TN, preferred_element_type=F32)
        qe = jnp.dot(qb, e_mat, preferred_element_type=F32)
        return jnp.sum(
            qe * sel[span(b, group_rows), :].astype(F32), axis=0, keepdims=True
        )

    def coarse_end(c_ref, to_ref):
        to_ref[...] = (
            (csum[...] + prior * c_ref[...].astype(F32)) / (cmass[:, :1] + prior)
        ).astype(BF)

    loads[2].wait()
    half_first = half_row_of(coarse_ref)
    csum[...] = jnp.zeros_like(csum)
    cmass[...] = jnp.zeros_like(cmass)

    def prep(b):
        rows_g = rows_of(b)
        ids_t = jnp.transpose(
            ids_all[pl.ds(b * planes, planes)].reshape(per_group * 8, 128).astype(F32)
        )
        hits = []
        for s in range(per_group):
            hit = jnp.zeros((per_sender, coarse_n), jnp.bool_)
            for k in range(MOST):
                hit = hit | (ids_t[:per_sender, s * 8 + k : s * 8 + k + 1] == row_lane)
            hits.append(hit.astype(F32))
        hit = jnp.concatenate(hits, axis=0)
        match[span(b, group_rows), :] = hit
        ranks = []
        for i in range(group_rows // step):
            m = hit[i * step : (i + 1) * step]
            upto = jnp.dot(lower, m.astype(BF), preferred_element_type=F32)
            ranks.append((upto * m).astype(BF))
        rank = jnp.concatenate(ranks, axis=0)
        rank_e = jnp.dot(rank, e_mat, preferred_element_type=F32)
        pick = ((rank_e == want) & same).astype(BF)
        sel[span(b, group_rows), :] = pick
        slots_g = lax.dot_general(pick, rows_g, TN, preferred_element_type=F32).astype(BF)
        arrived[span(b, 128), :] = slots_g
        slot_q = coarse_group(b, rows_g, coarse_ref, half_first, hit)
        sq_first[b] = jnp.broadcast_to(slot_q, (8, 128))

    cluster2 = jnp.concatenate([slot_cluster] * 2, axis=1)
    twice = lambda v: jnp.concatenate([v, v], axis=1)

    def pair_slots(b0, b1):
        return jnp.concatenate([arrived[span(b0, 128), :], arrived[span(b1, 128), :]], axis=0)

    def pair_prob(b0, b1):
        slots_g = pair_slots(b0, b1)
        tops, sums = [], []
        for part in parts:
            d = lax.dot_general(fine_ref[part, :], slots_g, NT, preferred_element_type=F32)
            l = jnp.where(
                twice(pcol[part, :]) == cluster2, (d - twice(norms[part, :])) * scale2, -jnp.inf
            )
            logit[part, :], top, total_e = tile_softmax(l)
            tops.append(top)
            sums.append(total_e)
        slot_q = jnp.concatenate([sq_first[b0][:1], sq_first[b1][:1]], axis=1)
        return tile_factors(tops, sums, slot_q)

    def pair_sum(i, b0, b1, factors):
        slots_g = pair_slots(b0, b1)
        for part, factor in zip(parts, factors):
            resp = logit[part, :] * factor
            fsum = jnp.dot(resp.astype(BF), slots_g, preferred_element_type=F32)
            mass = resp[:, :128] + resp[:, 128:]
            if i > 0:
                fsum = fsum + facc[part, :]
                mass = mass + masses[part, :]
            if i < groups // 2 - 1:
                facc[part, :] = fsum
                masses[part, :] = mass
            else:
                fine_ref[part, :] = (
                    (fsum + fine_ref[part, :].astype(F32))
                    * (1.0 / (jnp.sum(mass, axis=1, keepdims=True) + 1.0))
                ).astype(BF)
                outs.append(
                    pltpu.make_async_copy(
                        fine_ref.at[part, :], f1_out.at[part, :], out_sem.at[len(outs)]
                    )
                )
                outs[-1].start()

    def arrived_copy():
        outs.append(pltpu.make_async_copy(arrived, arrived_out, out_sem.at[len(outs)]))
        outs[-1].start()

    def fill_norms():
        loads[4].wait()
        for part in parts:
            ff = fine_ref[part, :].astype(F32)
            half = 0.5 * jnp.sum(ff * ff, axis=1, keepdims=True)
            norms[part, :] = jnp.broadcast_to(half, (tile, 128))

    last = nz + nx - 1
    if interleave:
        up = z < nz // 2
        order = [jnp.where(up, (z + k) % nz, (z - k + nz) % nz) for k in range(nz)]
        pairs = [(order[2 * i], order[2 * i + 1]) for i in range(nz // 2)]
        for t in range(1, last):
            comm_step(t)
            k = t - (nx - 1)
            if k == 0:
                fill_norms()
            if 0 <= k < nz // 2:
                wait_other(order[k])
                prep(order[k])
            elif k == nz // 2:
                pair_sum(0, *pairs[0], pair_prob(*pairs[0]))
                wait_other(order[k])
                prep(order[k])
        for k in range(nz // 2 + 1, nz):
            wait_other(order[k])
            prep(order[k])
        arrived_copy()
        for i in range(1, nz // 2):
            pair_sum(i, *pairs[i], pair_prob(*pairs[i]))
    else:
        fill_norms()
        for t in range(1, last):
            comm_step(t)
        for t in range(nz):
            each_z(t, lambda zc, _: wait_other(zc))
        lax.fori_loop(0, groups, lambda b, c: (prep(b), c)[1], 0)
        arrived_copy()
        for i in range(groups // 2):
            pair_sum(i, 2 * i, 2 * i + 1, pair_prob(2 * i, 2 * i + 1))

    coarse_end(coarse_ref, c1)
    half_second = half_row_of(c1)
    csum[...] = jnp.zeros_like(csum)
    cmass[...] = jnp.zeros_like(cmass)

    def second(b):
        slot_q = coarse_group(b, rows_of(b), c1, half_second, match[span(b, group_rows), :])
        sq_out[b] = jnp.broadcast_to(slot_q, (8, 128))

    if interleave:
        rows_g = rows_all[...].reshape(total, width)
        dots = lax.dot_general(rows_g, c1[...], NT, preferred_element_type=F32)
        masked = jnp.where(match[...] > 0.5, (dots - half_second) * scale, -jnp.inf)
        ex = jnp.exp(masked - jnp.max(masked, axis=1, keepdims=True))
        qb = (ex * (1.0 / jnp.sum(ex, axis=1, keepdims=True))).astype(BF)
        csum[...] = lax.dot_general(qb, rows_g, TN, preferred_element_type=F32)
        mass_row = jnp.sum(qb.astype(F32), axis=0, keepdims=True)
        mass_col = jnp.sum(jnp.where(ci == cj, mass_row, 0.0), axis=1, keepdims=True)
        cmass[...] = jnp.broadcast_to(mass_col, cmass.shape)
        qe = jnp.dot(qb, e_mat, preferred_element_type=F32) * sel[...].astype(F32)
        for b in range(groups):
            slot_q = jnp.sum(
                qe[b * group_rows : (b + 1) * group_rows], axis=0, keepdims=True
            )
            sq_out[b] = jnp.broadcast_to(slot_q, (8, 128))
    else:
        lax.fori_loop(0, groups, lambda b, c: (second(b), c)[1], 0)
    coarse_end(c1, c2_out)

    for src, dst in ((sq_out, sq_hbm), (c2_out, c2_hbm)):
        outs.append(pltpu.make_async_copy(src, dst, out_sem.at[len(outs)]))
        outs[-1].start()
    for c in outs:
        c.wait()
    def sent(zc, cc, way, ok):
        @pl.when(ok)
        def _():
            for c in copies(zc, cc, way, here(z, other)):
                c.wait_send()
    for zc in range(nz):
        sent(zc, ce, 1, (zc <= z) & (z < nz - 1))
        sent(zc, ce, 0, (zc >= z) & (z > 0))
        for xc in range(nx):
            cc = xc * 2 + core
            sent(zc, cc, 3, (xc <= x) & (x < nx - 1))
            sent(zc, cc, 2, (xc >= x) & (x > 0))
            sent(zc, cc, 4, true)


def first(nz, nc, rows, ids, parent, fine, coarse):
    per_sender, width = rows.shape
    senders = nz * nc
    total = senders * per_sender
    coarse_n = coarse.shape[0]
    block = fine.shape[0]
    owned = coarse_n // senders
    slots = senders * owned * MOST
    groups = slots // 128
    return pl.pallas_call(
        functools.partial(first_kernel, nz, nc, owned),
        out_shape=(
            jax.ShapeDtypeStruct(fine.shape, BF),
            jax.ShapeDtypeStruct((slots, width), BF),
            jax.ShapeDtypeStruct((block, 128), jnp.int32),
            jax.ShapeDtypeStruct((8, 128), jnp.int32),
            jax.ShapeDtypeStruct((groups, 8, 128), F32),
            jax.ShapeDtypeStruct(coarse.shape, BF),
        ),
        in_specs=[pl.BlockSpec(memory_space=pltpu.HBM)] * 5,
        out_specs=(pl.BlockSpec(memory_space=pltpu.HBM),) * 6,
        scratch_shapes=[
            pltpu.VMEM((slots, width), BF),
            pltpu.VMEM((block, 128), jnp.int32),
            pltpu.VMEM((8, 128), jnp.int32),
            pltpu.VMEM((groups, 8, 128), F32),
            pltpu.VMEM(coarse.shape, BF),
            pltpu.VMEM((nz, nc) + rows.shape, BF),
            pltpu.VMEM((nz, nc, 8, 128), jnp.int32),
            pltpu.VMEM((total, coarse_n), F32),
            pltpu.VMEM((total, 128), BF),
            pltpu.VMEM((block, 128), F32),
            pltpu.VMEM((block, 256), F32),
            pltpu.VMEM(fine.shape, F32),
            pltpu.VMEM((block, 128), F32),
            pltpu.VMEM(coarse.shape, F32),
            pltpu.VMEM((coarse_n, 128), F32),
            pltpu.VMEM(coarse.shape, BF),
            pltpu.VMEM((groups, 8, 128), F32),
            pltpu.VMEM(ids.shape, jnp.int32),
            pltpu.VMEM(parent.shape, jnp.int32),
            pltpu.VMEM(fine.shape, BF),
            pltpu.VMEM(coarse.shape, BF),
            pltpu.SemaphoreType.DMA((5, nz, nc)),
            pltpu.SemaphoreType.DMA((nz, nc)),
            pltpu.SemaphoreType.DMA((5, nz, nc)),
            pltpu.SemaphoreType.DMA((nz, nc)),
            pltpu.SemaphoreType.DMA((5,)),
            pltpu.SemaphoreType.DMA((5 + max(1, block // 512),)),
        ],
        compiler_params=pltpu.CompilerParams(
            collective_id=0,
            has_side_effects=True,
            vmem_limit_bytes=VMEM_LIMIT,
        ),
    )(rows, ids, parent, fine, coarse)


def second_kernel(
    f1_hbm, arrived_hbm, pcol_hbm, scl_hbm, sq_hbm, c2_hbm, fine_out, coarse_out,
    scl_ref, sq_ref, logit, result, f1_ref, arrived, pcol, sems, in_sems,
):
    block, width = f1_hbm.shape
    groups = sq_hbm.shape[0]
    slots = groups * 128
    scale2 = math.log2(math.e) / math.sqrt(width)
    tile = min(512, block)
    parts = [pl.ds(b * tile, tile) for b in range(block // tile)]
    small = [
        pltpu.make_async_copy(a, b, in_sems.at[i])
        for i, (a, b) in enumerate(
            [(arrived_hbm, arrived), (scl_hbm, scl_ref), (sq_hbm, sq_ref), (c2_hbm, coarse_out)]
        )
    ]
    for c in small:
        c.start()
    loads = []
    for b, part in enumerate(parts):
        loads.append(
            [
                pltpu.make_async_copy(src.at[part, :], dst.at[part, :], in_sems.at[4 + 2 * b + i])
                for i, (src, dst) in enumerate([(f1_hbm, f1_ref), (pcol_hbm, pcol)])
            ]
        )
        for c in loads[-1]:
            c.start()
    for c in small[:3]:
        c.wait()
    slot_cluster = jnp.concatenate([scl_ref[:1, :]] * groups, axis=1)
    slot_q = jnp.concatenate([sq_ref[b, :1, :] for b in range(groups)], axis=1)
    tops, sums = [], []
    for part, pending in zip(parts, loads):
        for c in pending:
            c.wait()
        ft = f1_ref[part, :]
        ff = ft.astype(F32)
        norm = 0.5 * jnp.sum(ff * ff, axis=1, keepdims=True)
        d = lax.dot_general(ft, arrived[...], NT, preferred_element_type=F32)
        same = jnp.concatenate([pcol[part, :]] * groups, axis=1) == slot_cluster
        l = jnp.where(same, (d - norm) * scale2, -jnp.inf)
        logit[part, :], top, total_e = tile_softmax(l)
        tops.append(top)
        sums.append(total_e)
    factors = tile_factors(tops, sums, slot_q)
    copies = [small[3]]
    for b, part in enumerate(parts):
        resp = logit[part, :] * factors[b]
        mass = jnp.sum(resp, axis=1, keepdims=True)
        fsum = jnp.dot(resp.astype(BF), arrived[...], preferred_element_type=F32)
        result[part, :] = (
            (fsum + f1_ref[part, :].astype(F32)) * (1.0 / (mass + 1.0))
        ).astype(BF)
        copies.append(pltpu.make_async_copy(result.at[part, :], fine_out.at[part, :], sems.at[b]))
        copies[-1].start()
    for c in copies:
        c.wait()


def second(f1, arrived, pcol, scl, sq, c2):
    block, width = f1.shape
    slots = arrived.shape[0]
    return pl.pallas_call(
        second_kernel,
        out_shape=(jax.ShapeDtypeStruct(f1.shape, BF), jax.ShapeDtypeStruct(c2.shape, BF)),
        in_specs=[pl.BlockSpec(memory_space=pltpu.HBM)] * 6,
        out_specs=(pl.BlockSpec(memory_space=pltpu.HBM),) * 2,
        scratch_shapes=[
            pltpu.VMEM(scl.shape, jnp.int32),
            pltpu.VMEM(sq.shape, F32),
            pltpu.VMEM((block, slots), F32),
            pltpu.VMEM((block, width), BF),
            pltpu.VMEM((block, width), BF),
            pltpu.VMEM((slots, width), BF),
            pltpu.VMEM((block, 128), jnp.int32),
            pltpu.SemaphoreType.DMA((max(1, block // 512),)),
            pltpu.SemaphoreType.DMA((4 + 2 * max(1, block // 512),)),
        ],
        compiler_params=pltpu.CompilerParams(vmem_limit_bytes=VMEM_LIMIT),
    )(f1, arrived, pcol, scl, sq, c2)


def on_device(rows, coarse_ids, parent, fine_cent, coarse_cent):
    nz = lax.axis_size("dp")
    nc = lax.axis_size("cent")
    return second(*first(nz, nc, rows, coarse_ids.T, parent.reshape(-1, 128), fine_cent, coarse_cent))


def solution(mesh):
    in_specs = (
        P(("groups", "dp", "cent"), None),
        P(("groups", "dp", "cent"), None),
        P("groups"),
        P(("groups", "dp", "cent"), None),
        P("groups", None),
    )
    out_specs = (P(("groups", "dp", "cent"), None), P("groups", None))
    return jax.shard_map(
        on_device, mesh=mesh, in_specs=in_specs, out_specs=out_specs, check_vma=False
    )
```
